32 devices in a mesh: grp: 4 (over y, core), shard: 4 (over z), side: 2 (over x).
Axes of the slice: x: 2, y: 2, z: 4, core: 2. Of those that a mesh axis runs over, the one named last changes fastest.
Arguments:
- tokens: bfloat16 [512, 4096], P(('grp', 'side')), may hold values from -6 to 6
- routes: int32 [512, 2], P(('grp', 'side')), may hold values from 0 to 3, all different within a row; in each aligned block of 64 rows (0 to 63, 64 to 127, ...) at most 64 rows name the same one
- probs: float32 [512, 2], P(('grp', 'side')), may hold values from 0.02 to 1
- w_gate: bfloat16 [16, 4096, 256], P(('grp', 'shard')), may hold values from -0.09375 to 0.09375
- w_up: bfloat16 [16, 4096, 256], P(('grp', 'shard')), may hold values from -0.09375 to 0.09375
- w_down: bfloat16 [16, 256, 4096], P(('grp', 'shard')), may hold values from -0.1875 to 0.1875
Outputs:
- mixed: bfloat16 [512, 4096], P(('grp', 'side'), 'shard')
The draws below stay inside these ranges and needn't reach their ends.
Inputs may be any that keep to these rules, and one draw needn't show every extreme that they name: `routes`: each token names 2 different experts. Within each aligned block of 64 tokens no expert is named by more than 64 tokens, a bound that some block reaches.
All inputs are finite; a program needn't handle non-finite values.
Results may differ from the reference program's by a relative error of at most 0.0057.
Values may be sent and summed in bfloat16 or wider, within the bound.
A program may use at most 64 MiB of HBM per device.

```python
import math
import jax
import jax.numpy as jnp
import numpy as np
from jax import lax

D = 4096
FF = 1024
TPE = 4
TILE_FF = 256
EXPERTS = 4
TOP = 2
TOK_GS = 64
CAP = 64
TOKENS = 512
ROWMAX = 512


def block_levels(key, extent, cuts, low, largest):
    gain = 1.0
    for dim, blocks in cuts:
        heights = jax.random.uniform(jax.random.fold_in(jax.random.fold_in(key, 6), dim), (blocks,), jnp.float32, low / len(cuts), largest / len(cuts))
        gain = gain * jnp.repeat(jnp.exp(heights), extent[dim] // blocks).reshape((-1,) + (1,) * (len(extent) - 1 - dim))
    return gain


def shared_out(key, own, number, rows, count, top, most, slope):
    sequence = jax.random.permutation(key, count)
    crowded, ordinary = portions_of(count, rows * top, most, slope, True), portions_of(count, rows * top, most, slope, False)
    places = jnp.arange(count)

    def named(sizes, rotation):
        used = int((sizes > 0).sum())
        fixed = max(1, used // 4)
        moved = fixed + (places - fixed + rotation * (used - fixed)) % max(1, count - fixed)
        return jnp.zeros((count,), jnp.int32).at[sequence[jnp.where(places < fixed, places, moved)]].set(jnp.asarray(sizes, jnp.int32))

    sizes = jnp.where(number % 4 == 0, named(crowded, number // 4), named(ordinary, number - number // 4 - 1))
    mixed = jax.random.permutation(jax.random.fold_in(own, 3), count)
    donor, sink = mixed[0:count // 2 * 2:2], mixed[1:count // 2 * 2:2]
    slack = jnp.minimum(sizes[donor] - 1, most - sizes[sink]) // 2
    slack = jnp.where((donor == sequence[0]) | (sink == sequence[0]) | (sizes[sink] == 0), 0, jnp.maximum(slack, 0))
    moved = jax.random.randint(jax.random.fold_in(own, 4), (count // 2,), 0, 1 << 20) % (slack + 1)
    sizes = sizes.at[donor].add(-moved).at[sink].add(moved)
    labels = jnp.searchsorted(jnp.cumsum(sizes), jnp.arange(rows * top), side="right").astype(jnp.int32)
    table = labels.reshape(top, rows).T
    table = table[jax.random.permutation(jax.random.fold_in(own, 1), rows)]
    rotation = jax.random.randint(jax.random.fold_in(own, 2), (rows, 1), 0, top)
    return jnp.take_along_axis(table, (jnp.arange(top)[None, :] + rotation) % top, axis=1)


def portions_of(number_of, total, limit, lean, full):
    weights = [(1 << 20) // math.isqrt(grade ** lean) + 1 for grade in range(1, number_of + 1)]
    largest = limit if full else min(limit, max(-(-total // number_of), total * weights[0] // sum(weights)))
    least = 1 if total - largest >= number_of - 1 else 0
    given, surplus = [largest] + [least] * (number_of - 1), total - largest - least * (number_of - 1)
    while surplus > 0:
        free = [i for i in range(1, number_of) if given[i] < largest] or [i for i in range(1, number_of) if given[i] < limit]
        whole, budget = sum([weights[i] for i in free]), surplus
        for i in free:
            more = min(limit - given[i], max(1, budget * weights[i] // whole), surplus)
            given[i] = given[i] + more
            surplus = surplus - more
    return np.array(given)


def noise(own_key, extent, scale, most, split=(), held_as=jnp.bfloat16):
    values = scale * jax.random.normal(own_key, extent, jnp.float32)
    if split:
        values = values * block_levels(own_key, extent, split, -0.22, 0.18)
    return jnp.clip(values, -most, most).astype(held_as)


def setup_inputs(seed: int = 0) -> dict:
    splits = jax.random.split(jax.random.key(seed), 7)
    tokens = noise(splits[0], (TOKENS, D), 1.0, 6.0, ((0, 8),))
    routes_keys = jax.random.split(jax.random.fold_in(splits[1], 1), TOKENS // TOK_GS)
    routes_turns = jax.random.permutation(jax.random.fold_in(splits[1], 3), TOKENS // TOK_GS)
    routes = jax.vmap(lambda own, number: shared_out(jax.random.fold_in(splits[1], 2), own, number, TOK_GS, EXPERTS, TOP, CAP, 2))(routes_keys, routes_turns).reshape((TOKENS, TOP))
    probs = jnp.clip(jnp.exp(math.log(1.0) - 3.912023 * jax.random.uniform(splits[2], (TOKENS, TOP), jnp.float32) ** block_levels(splits[2], (TOKENS, TOP), ((0, 8),), -0.2, 0.2)), 0.02, 1.0)
    w_gate = noise(splits[3], (EXPERTS * TPE, D, TILE_FF), D ** -0.5, 0.09375, ((0, 16),))
    w_up = noise(splits[4], (EXPERTS * TPE, D, TILE_FF), D ** -0.5, 0.09375, ((0, 16),))
    w_down = noise(splits[5], (EXPERTS * TPE, TILE_FF, D), FF ** -0.5, 0.1875, ((0, 16),))
    return {"tokens": tokens, "routes": routes, "probs": probs, "w_gate": w_gate, "w_up": w_up, "w_down": w_down}


def reference(tokens, routes, probs, w_gate, w_up, w_down):
    gates = probs / jnp.sum(probs, axis=-1, keepdims=True)
    gate_tiles = w_gate.reshape(EXPERTS, TPE, D, TILE_FF)
    up_tiles = w_up.reshape(EXPERTS, TPE, D, TILE_FF)
    down_tiles = w_down.reshape(EXPERTS, TPE, TILE_FF, D)
    positions = jnp.arange(ROWMAX)

    def one_expert(expert, total):
        match = routes == expert
        chosen = jnp.any(match, axis=1)
        weight = jnp.sum(jnp.where(match, gates, jnp.float32(0.0)), axis=1)
        index = jnp.nonzero(chosen, size=ROWMAX, fill_value=0)[0].astype(jnp.int32)
        valid = positions < jnp.sum(chosen.astype(jnp.int32))
        rows = tokens[index]
        summed = jnp.zeros((ROWMAX, D), jnp.float32)
        for tile in range(TPE):
            gate = jnp.dot(rows, gate_tiles[expert, tile], preferred_element_type=jnp.float32)
            upper = jnp.dot(rows, up_tiles[expert, tile], preferred_element_type=jnp.float32)
            hidden = (jax.nn.silu(gate) * upper).astype(jnp.bfloat16)
            part = jnp.dot(hidden, down_tiles[expert, tile], preferred_element_type=jnp.float32).astype(jnp.bfloat16)
            summed = summed + part.astype(jnp.float32)
        scale = jnp.where(valid, weight[index], jnp.float32(0.0))
        return total.at[index].add(summed * scale[:, None])

    total = lax.fori_loop(0, EXPERTS, one_expert, jnp.zeros((TOKENS, D), jnp.float32))
    return total.astype(jnp.bfloat16)
```

```python
import functools

import jax
import jax.numpy as jnp
from jax import lax
from jax.experimental import pallas as pl
from jax.experimental.pallas import tpu as pltpu
from jax.sharding import PartitionSpec as P

TPE = 4
CHUNK = 16
MESH = pl.DeviceIdType.MESH


def tile_pass(rows, w_gate, w_up, w_down):
    flat = rows.reshape(-1, rows.shape[2])
    gate = jnp.dot(flat, w_gate[0], preferred_element_type=jnp.float32)
    upper = jnp.dot(flat, w_up[0], preferred_element_type=jnp.float32)
    hidden = (jax.nn.silu(gate) * upper).astype(jnp.bfloat16)
    result = jnp.dot(hidden, w_down[0], preferred_element_type=jnp.float32).astype(jnp.bfloat16)
    return result.reshape(rows.shape[0], rows.shape[1], -1)


def on_device(tokens, routes, probs, w_gate, w_up, w_down):
    groups = lax.axis_size("grp")
    shards = lax.axis_size("shard")
    per_group = shards // TPE
    experts_all = groups * per_group
    tok_count = tokens.shape[0]
    top_count = routes.shape[1]
    capacity = 2 * tok_count * top_count // experts_all
    local = lax.axis_index("shard") // TPE
    targets = jnp.arange(groups, dtype=jnp.int32) * per_group + local
    gates = probs / jnp.sum(probs, axis=-1, keepdims=True)
    match = routes[:, :, None] == targets[None, None, :]
    hits = jnp.sum(match.astype(jnp.int32), axis=1)
    gate_hits = jnp.sum(jnp.where(match, gates[:, :, None], jnp.float32(0.0)), axis=1)
    ranks = jnp.cumsum(hits, axis=0) - 1
    slots = jnp.arange(capacity, dtype=jnp.int32)
    select = ((hits.T[:, None, :] > 0) & (ranks.T[:, None, :] == slots[None, :, None])).astype(
        jnp.bfloat16
    )
    outgoing = jnp.einsum("gct,td->gcd", select, tokens, preferred_element_type=jnp.float32).astype(
        jnp.bfloat16
    )
    arrived = lax.all_to_all(outgoing, "grp", split_axis=0, concat_axis=0, tiled=True)
    results = tile_pass(arrived, w_gate, w_up, w_down)
    returned = lax.all_to_all(results, "grp", split_axis=0, concat_axis=0, tiled=True)

    def add_group(total, items):
        picks, rows_back, weight = items
        picked = jnp.einsum("ct,cd->td", picks, rows_back, preferred_element_type=jnp.float32)
        return (total + weight[:, None] * picked, None)

    start = jnp.zeros((tok_count, tokens.shape[1]), jnp.float32)
    combined, unused = lax.scan(add_group, start, (select, returned, gate_hits.T))
    return lax.psum_scatter(combined, "shard", scatter_dimension=1, tiled=True).astype(jnp.bfloat16)


def dense_kernel(
    groups, shards, tokens, routes, probs, wg_hbm, wu_hbm, wd_hbm, out,
    x, gt, wg, wu, wd, own, cross, lend, borrowed, y_out, y_in, z_out, z_in, local_sem, send_sem, recv_sem,
):
    chunks, rows_per, width = tokens.shape
    half = chunks // 2
    rows = chunks * rows_per
    depth = wg.shape[0]
    grp, z = lax.axis_index("grp"), lax.axis_index("shard")
    odd = lax.rem(z, 2)
    sibling = {"grp": grp + 1 - 2 * lax.rem(grp, 2)}
    over = lax.rem(grp + 2, groups)
    across = {"grp": over}
    diagonal = {"grp": over + 1 - 2 * lax.rem(over, 2)}
    pair = {"shard": z + 1 - 2 * odd}
    rest = [{"shard": lax.rem(z + d, shards)} for d in range(1, shards)]

    loads = [
        pltpu.make_async_copy(wg_hbm.at[0], wg, local_sem.at[0]),
        pltpu.make_async_copy(wu_hbm.at[0], wu, local_sem.at[1]),
        pltpu.make_async_copy(wd_hbm.at[0], wd, local_sem.at[2]),
    ]
    starts = [half * odd, half * (1 - odd)]
    loads += [
        pltpu.make_async_copy(tokens.at[pl.ds(starts[i], half)], x.at[0, pl.ds(i * half, half)], local_sem.at[3 + i])
        for i in range(2)
    ]
    for load in loads:
        load.start()

    barrier = pltpu.get_barrier_semaphore()
    greeted = [sibling, across, diagonal] + rest
    for device in greeted:
        pl.semaphore_signal(barrier, inc=1, device_id=device, device_id_type=MESH)

    share = probs[...] / jnp.sum(probs[...], axis=1, keepdims=True)
    row_at = lax.rem(lax.broadcasted_iota(jnp.int32, (rows, gt.shape[2]), 0) + half * rows_per * odd, rows)
    diag = row_at == lax.broadcasted_iota(jnp.int32, (rows, gt.shape[2]), 1)
    gt[0] = jnp.zeros(gt.shape[1:], jnp.float32)
    for expert in range(groups):
        column = jnp.sum(jnp.where(routes[...] == expert, share, 0.0), axis=1, keepdims=True)
        gt[0, expert : expert + 1, :] = jnp.sum(jnp.where(diag, column, 0.0), axis=0, keepdims=True)

    pl.semaphore_wait(barrier, len(greeted))

    number = [0]

    def remote(from_ref, to_ref, device):
        at = number[0]
        number[0] += 1
        return pltpu.make_async_remote_copy(
            src_ref=from_ref, dst_ref=to_ref, send_sem=send_sem.at[at], recv_sem=recv_sem.at[at],
            device_id=device, device_id_type=MESH,
        )

    sent = []

    def begin(copy):
        copy.start()
        sent.append(copy)
        return copy

    direct = [begin(remote(tokens.at[half * odd + k], x.at[2, k], across)) for k in range(half)]
    beside = [
        begin(remote(tokens.at[pl.ds(starts[i], half)], x.at[1, pl.ds(i * half, half)], sibling)) for i in range(2)
    ]
    gate_copies = [
        begin(remote(gt.at[0], gt.at[slot], device))
        for slot, device in ((1, sibling), (2, across), (3, diagonal))
    ]
    paired = [remote(x.at[2, k], x.at[2, half + k], pair) for k in range(half)]
    passed = [remote(x.at[2, k], x.at[3, k], sibling) for k in range(chunks)]
    lent_home = remote(lend.at[0], borrowed.at[0], sibling)
    lent_away = [
        remote(lend.at[1, pl.ds(i * half, half)], borrowed.at[1, pl.ds(i * half, half)], sibling) for i in range(2)
    ]
    y_copies = [remote(y_out.at[r], y_in.at[r], across) for r in range(chunks)]
    z_base = number[0]

    def z_copy(step, r, to_index):
        return pltpu.make_async_remote_copy(
            src_ref=z_out.at[r, lax.rem(z + step, shards)],
            dst_ref=z_in.at[step - 1, to_index],
            send_sem=send_sem.at[z_base + (step - 1) * chunks + r],
            recv_sem=recv_sem.at[z_base + (step - 1) * chunks + to_index],
            device_id=rest[step - 1],
            device_id_type=MESH,
        )

    def gate_column(slot, first, count):
        picked = jnp.where(lax.broadcasted_iota(jnp.int32, gt.shape[1:], 0) == grp, gt[slot], 0.0)
        line = jnp.sum(picked, axis=0, keepdims=True)
        at = lax.broadcasted_iota(jnp.int32, (count, gt.shape[2]), 0) + first
        return jnp.sum(
            jnp.where(at == lax.broadcasted_iota(jnp.int32, (count, gt.shape[2]), 1), line, 0.0), axis=1, keepdims=True
        )

    def experts(slot, first, count, kept, given):
        each = count * rows_per
        steps = 4
        span = depth // steps
        gate = jnp.zeros((2 * each, wg.shape[1]), jnp.float32)
        upper = jnp.zeros((2 * each, wg.shape[1]), jnp.float32)
        for step in range(steps):
            piece = x[slot : slot + 2, first : first + count, :, step * span : (step + 1) * span]
            piece = piece.reshape(2 * each, span)
            gate += jnp.dot(piece, wg[step * span : (step + 1) * span, :], preferred_element_type=jnp.float32)
            upper += jnp.dot(piece, wu[step * span : (step + 1) * span, :], preferred_element_type=jnp.float32)
        hidden = (gate / (1.0 + jnp.exp(-gate)) * upper).astype(jnp.bfloat16)
        scale = jnp.concatenate(
            [gate_column(slot, first * rows_per, each), gate_column(slot + 1, first * rows_per, each)], axis=0
        )
        cw = width // shards
        for q in range(shards):
            part = jnp.dot(hidden, wd[:, q * cw : (q + 1) * cw], preferred_element_type=jnp.float32) * scale
            kept[first : first + count, q] = part[:each].reshape(count, rows_per, cw)
            lend[given, first : first + count, q] = part[each:].astype(jnp.bfloat16).reshape(count, rows_per, cw)

    def arrive(k):
        direct[k].wait_recv()
        begin(paired[k])
        begin(passed[k])

    def arrive_pair(k):
        paired[k].wait_recv()
        begin(passed[half + k])

    def to_across(part):
        lent_away[part].wait_recv()
        for r in range(part * half, (part + 1) * half):
            y_out[r] = (cross[r] + borrowed[1, r].astype(jnp.float32)).astype(jnp.bfloat16)
            begin(y_copies[r])

    for k in range(half - 1):
        arrive(k)
    for load in loads:
        load.wait()
    for copy in beside + gate_copies:
        copy.wait_recv()
    experts(0, 0, chunks, own, 0)
    begin(lent_home)
    arrive(half - 1)
    for k in range(half - 1):
        arrive_pair(k)
    for r in range(half):
        passed[r].wait_recv()
    experts(2, 0, half, cross, 1)
    begin(lent_away[0])
    arrive_pair(half - 1)
    to_across(0)
    for r in range(half, chunks):
        passed[r].wait_recv()
    experts(2, half, half, cross, 1)
    begin(lent_away[1])
    to_across(1)

    lent_home.wait_recv()
    for r in range(chunks):
        y_copies[r].wait_recv()
        total = own[r] + borrowed[0, r].astype(jnp.float32) + y_in[r].astype(jnp.float32)
        own[r] = total
        z_out[r] = total.astype(jnp.bfloat16)
        for step in range(1, shards):
            begin(z_copy(step, r, lax.rem(r + half * lax.rem(step, 2), chunks)))
    for r in range(chunks):
        total = own[r, z]
        for step in range(1, shards):
            z_copy(step, r, r).wait_recv()
            total = total + z_in[step - 1, r].astype(jnp.float32)
        out[lax.rem(r + half * odd, chunks)] = total.astype(jnp.bfloat16)
    for copy in sent:
        copy.wait_send()


def dense_on_device(tokens, routes, probs, w_gate, w_up, w_down):
    groups, shards = lax.axis_size("grp"), lax.axis_size("shard")
    tok_count, width = tokens.shape
    depth, tile = w_gate.shape[1:]
    chunks, cw = tok_count // CHUNK, width // shards
    half = chunks // 2
    copies = half + 2 + 3 + half + chunks + 1 + 2 + chunks + (shards - 1) * chunks
    lanes = -(-tok_count // 128) * 128
    bf16, f32 = jnp.bfloat16, jnp.float32
    block = (chunks, shards, CHUNK, cw)
    whole = pl.BlockSpec(memory_space=pltpu.VMEM)
    away = pl.BlockSpec(memory_space=pl.ANY)
    total_rows = groups * tok_count
    mixed = pl.pallas_call(
        functools.partial(dense_kernel, groups, shards),
        out_shape=jax.ShapeDtypeStruct((chunks, CHUNK, cw), bf16),
        in_specs=[away, whole, whole, away, away, away],
        out_specs=whole,
        scratch_shapes=[
            pltpu.VMEM((4, chunks, CHUNK, width), bf16),
            pltpu.VMEM((4, -(-groups // 8) * 8, lanes), f32),
            pltpu.VMEM((depth, tile), bf16),
            pltpu.VMEM((depth, tile), bf16),
            pltpu.VMEM((tile, width), bf16),
            pltpu.VMEM(block, f32),
            pltpu.VMEM(block, f32),
            pltpu.VMEM((2,) + block, bf16),
            pltpu.VMEM((2,) + block, bf16),
            pltpu.VMEM(block, bf16),
            pltpu.VMEM(block, bf16),
            pltpu.VMEM(block, bf16),
            pltpu.VMEM((shards - 1, chunks, CHUNK, cw), bf16),
            pltpu.SemaphoreType.DMA((5,)),
            pltpu.SemaphoreType.DMA((copies,)),
            pltpu.SemaphoreType.DMA((copies,)),
        ],
        compiler_params=pltpu.CompilerParams(
            collective_id=0, has_side_effects=True, vmem_limit_bytes=40 * 1024 * 1024
        ),
        cost_estimate=pl.CostEstimate(
            flops=6 * total_rows * depth * tile, bytes_accessed=6 * depth * tile, transcendentals=total_rows * tile
        ),
    )(tokens.reshape(chunks, CHUNK, width), routes, probs, w_gate, w_up, w_down)
    return mixed.reshape(tok_count, cw)


def is_dense(mesh, tokens, routes):
    groups, shards, sides = mesh.shape["grp"], mesh.shape["shard"], mesh.shape["side"]
    tok_count = tokens.shape[0] // (groups * sides)
    per_group = shards // TPE
    capacity = 2 * tok_count * routes.shape[1] // (groups * per_group)
    return groups == 4 and per_group == 1 and capacity >= tok_count and tok_count % (2 * CHUNK) == 0


def solution(mesh):
    def call(tokens, routes, probs, w_gate, w_up, w_down):
        body = dense_on_device if is_dense(mesh, tokens, routes) else on_device
        return jax.shard_map(
            body,
            mesh=mesh,
            in_specs=(
                P(("grp", "side"), None),
                P(("grp", "side"), None),
                P(("grp", "side"), None),
                P(("grp", "shard"), None, None),
                P(("grp", "shard"), None, None),
                P(("grp", "shard"), None, None),
            ),
            out_specs=P(("grp", "side"), "shard"),
            check_vma=False,
        )(tokens, routes, probs, w_gate, w_up, w_down)

    return call
```

```python
import functools

import jax
import jax.numpy as jnp
from jax import lax
from jax.experimental import pallas as pl
from jax.experimental.pallas import tpu as pltpu
from jax.sharding import PartitionSpec as P

TPE = 4
CHUNK = 16
MESH = pl.DeviceIdType.MESH


def tile_pass(rows, w_gate, w_up, w_down):
    flat = rows.reshape(-1, rows.shape[2])
    gate = jnp.dot(flat, w_gate[0], preferred_element_type=jnp.float32)
    upper = jnp.dot(flat, w_up[0], preferred_element_type=jnp.float32)
    hidden = (jax.nn.silu(gate) * upper).astype(jnp.bfloat16)
    result = jnp.dot(hidden, w_down[0], preferred_element_type=jnp.float32).astype(jnp.bfloat16)
    return result.reshape(rows.shape[0], rows.shape[1], -1)


def on_device(tokens, routes, probs, w_gate, w_up, w_down):
    groups = lax.axis_size("grp")
    shards = lax.axis_size("shard")
    per_group = shards // TPE
    experts_all = groups * per_group
    tok_count = tokens.shape[0]
    top_count = routes.shape[1]
    capacity = 2 * tok_count * top_count // experts_all
    local = lax.axis_index("shard") // TPE
    targets = jnp.arange(groups, dtype=jnp.int32) * per_group + local
    gates = probs / jnp.sum(probs, axis=-1, keepdims=True)
    match = routes[:, :, None] == targets[None, None, :]
    hits = jnp.sum(match.astype(jnp.int32), axis=1)
    gate_hits = jnp.sum(jnp.where(match, gates[:, :, None], jnp.float32(0.0)), axis=1)
    ranks = jnp.cumsum(hits, axis=0) - 1
    slots = jnp.arange(capacity, dtype=jnp.int32)
    select = ((hits.T[:, None, :] > 0) & (ranks.T[:, None, :] == slots[None, :, None])).astype(
        jnp.bfloat16
    )
    outgoing = jnp.einsum("gct,td->gcd", select, tokens, preferred_element_type=jnp.float32).astype(
        jnp.bfloat16
    )
    arrived = lax.all_to_all(outgoing, "grp", split_axis=0, concat_axis=0, tiled=True)
    results = tile_pass(arrived, w_gate, w_up, w_down)
    returned = lax.all_to_all(results, "grp", split_axis=0, concat_axis=0, tiled=True)

    def add_group(total, items):
        picks, rows_back, weight = items
        picked = jnp.einsum("ct,cd->td", picks, rows_back, preferred_element_type=jnp.float32)
        return (total + weight[:, None] * picked, None)

    start = jnp.zeros((tok_count, tokens.shape[1]), jnp.float32)
    combined, unused = lax.scan(add_group, start, (select, returned, gate_hits.T))
    return lax.psum_scatter(combined, "shard", scatter_dimension=1, tiled=True).astype(jnp.bfloat16)


def dense_kernel(
    groups, shards, tokens, routes, probs, wg_hbm, wu_hbm, wd_hbm, out,
    x, gt, wg, wu, wd, own, cross, lend, borrowed, y_out, y_in, z_out, z_in, local_sem, send_sem, recv_sem,
):
    chunks, rows_per, width = tokens.shape
    half = chunks // 2
    rows = chunks * rows_per
    depth = wg.shape[0]
    grp, z = lax.axis_index("grp"), lax.axis_index("shard")
    odd = lax.rem(z, 2)
    sibling = {"grp": grp + 1 - 2 * lax.rem(grp, 2)}
    over = lax.rem(grp + 2, groups)
    across = {"grp": over}
    diagonal = {"grp": over + 1 - 2 * lax.rem(over, 2)}
    pair = {"shard": z + 1 - 2 * odd}
    rest = [{"shard": lax.rem(z + d, shards)} for d in range(1, shards)]

    loads = [
        pltpu.make_async_copy(wg_hbm.at[0], wg, local_sem.at[0]),
        pltpu.make_async_copy(wu_hbm.at[0], wu, local_sem.at[1]),
        pltpu.make_async_copy(wd_hbm.at[0], wd, local_sem.at[2]),
    ]
    starts = [half * odd, half * (1 - odd)]
    loads += [
        pltpu.make_async_copy(tokens.at[pl.ds(starts[i], half)], x.at[0, pl.ds(i * half, half)], local_sem.at[3 + i])
        for i in range(2)
    ]
    for load in loads:
        load.start()

    barrier = pltpu.get_barrier_semaphore()
    greeted = [sibling, across, diagonal] + rest
    for device in greeted:
        pl.semaphore_signal(barrier, inc=1, device_id=device, device_id_type=MESH)

    share = probs[...] / jnp.sum(probs[...], axis=0, keepdims=True)
    gt[0] = jnp.zeros(gt.shape[1:], jnp.float32)
    for expert in range(groups):
        line = jnp.sum(jnp.where(routes[...] == expert, share, 0.0), axis=0, keepdims=True)
        gt[0, expert : expert + 1, 0:rows] = line

    pl.semaphore_wait(barrier, len(greeted))

    number = [0]

    def remote(from_ref, to_ref, device):
        at = number[0]
        number[0] += 1
        return pltpu.make_async_remote_copy(
            src_ref=from_ref, dst_ref=to_ref, send_sem=send_sem.at[at], recv_sem=recv_sem.at[at],
            device_id=device, device_id_type=MESH,
        )

    sent = []

    def begin(copy):
        copy.start()
        sent.append(copy)
        return copy

    direct = [begin(remote(tokens.at[half * odd + k], x.at[2, k], across)) for k in range(half)]
    beside = [
        begin(remote(tokens.at[pl.ds(starts[i], half)], x.at[1, pl.ds(i * half, half)], sibling)) for i in range(2)
    ]
    gate_copies = [
        begin(remote(gt.at[0], gt.at[slot], device))
        for slot, device in ((1, sibling), (2, across), (3, diagonal))
    ]
    paired = [remote(x.at[2, k], x.at[2, half + k], pair) for k in range(half)]
    passed = [remote(x.at[2, k], x.at[3, k], sibling) for k in range(chunks)]
    lent_home = remote(lend.at[0], borrowed.at[0], sibling)
    lent_away = [
        remote(lend.at[1, pl.ds(i * half, half)], borrowed.at[1, pl.ds(i * half, half)], sibling) for i in range(2)
    ]
    y_copies = [remote(y_out.at[r], y_in.at[r], across) for r in range(chunks)]
    z_base = number[0]

    def z_copy(step, r, to_index):
        return pltpu.make_async_remote_copy(
            src_ref=z_out.at[r, lax.rem(z + step, shards)],
            dst_ref=z_in.at[step - 1, to_index],
            send_sem=send_sem.at[z_base + (step - 1) * chunks + r],
            recv_sem=recv_sem.at[z_base + (step - 1) * chunks + to_index],
            device_id=rest[step - 1],
            device_id_type=MESH,
        )

    def gate_column(slot, first, count):
        picked = jnp.where(lax.broadcasted_iota(jnp.int32, gt.shape[1:], 0) == grp, gt[slot], 0.0)
        line = jnp.sum(picked, axis=0, keepdims=True)
        at = lax.broadcasted_iota(jnp.int32, (count, gt.shape[2]), 0) + (first + half * rows_per * odd)
        at = lax.rem(at, rows)
        return jnp.sum(
            jnp.where(at == lax.broadcasted_iota(jnp.int32, (count, gt.shape[2]), 1), line, 0.0), axis=1, keepdims=True
        )

    def experts(slot, first, count, kept, given):
        each = count * rows_per
        steps = 4
        span = depth // steps
        gate = jnp.zeros((2 * each, wg.shape[1]), jnp.float32)
        upper = jnp.zeros((2 * each, wg.shape[1]), jnp.float32)
        for step in range(steps):
            piece = x[slot : slot + 2, first : first + count, :, step * span : (step + 1) * span]
            piece = piece.reshape(2 * each, span)
            gate += jnp.dot(piece, wg[step * span : (step + 1) * span, :], preferred_element_type=jnp.float32)
            upper += jnp.dot(piece, wu[step * span : (step + 1) * span, :], preferred_element_type=jnp.float32)
        hidden = (gate / (1.0 + jnp.exp(-gate)) * upper).astype(jnp.bfloat16)
        scale = jnp.concatenate(
            [gate_column(slot, first * rows_per, each), gate_column(slot + 1, first * rows_per, each)], axis=0
        )
        cw = width // shards
        for q in range(shards):
            part = jnp.dot(hidden, wd[:, q * cw : (q + 1) * cw], preferred_element_type=jnp.float32) * scale
            kept[first : first + count, q] = part[:each].reshape(count, rows_per, cw)
            lend[given, first : first + count, q] = part[each:].astype(jnp.bfloat16).reshape(count, rows_per, cw)

    def arrive(k):
        direct[k].wait_recv()
        begin(paired[k])
        begin(passed[k])

    def arrive_pair(k):
        paired[k].wait_recv()
        begin(passed[half + k])

    def to_across(part):
        lent_away[part].wait_recv()
        for r in range(part * half, (part + 1) * half):
            y_out[r] = (cross[r] + borrowed[1, r].astype(jnp.float32)).astype(jnp.bfloat16)
            begin(y_copies[r])

    for k in range(half - 1):
        arrive(k)
    for load in loads:
        load.wait()
    for copy in beside + gate_copies:
        copy.wait_recv()
    experts(0, 0, chunks, own, 0)
    begin(lent_home)
    arrive(half - 1)
    for k in range(half - 1):
        arrive_pair(k)
    for r in range(half):
        passed[r].wait_recv()
    experts(2, 0, half, cross, 1)
    begin(lent_away[0])
    arrive_pair(half - 1)
    to_across(0)
    for r in range(half, chunks):
        passed[r].wait_recv()
    experts(2, half, half, cross, 1)
    begin(lent_away[1])
    to_across(1)

    lent_home.wait_recv()
    for r in range(chunks):
        y_copies[r].wait_recv()
        total = own[r] + borrowed[0, r].astype(jnp.float32) + y_in[r].astype(jnp.float32)
        own[r] = total
        z_out[r] = total.astype(jnp.bfloat16)
        for step in range(1, shards):
            begin(z_copy(step, r, lax.rem(r + half * lax.rem(step, 2), chunks)))
    for r in range(chunks):
        total = own[r, z]
        for step in range(1, shards):
            z_copy(step, r, r).wait_recv()
            total = total + z_in[step - 1, r].astype(jnp.float32)
        out[lax.rem(r + half * odd, chunks)] = total.astype(jnp.bfloat16)
    for copy in sent:
        copy.wait_send()


def dense_on_device(tokens, routes, probs, w_gate, w_up, w_down):
    groups, shards = lax.axis_size("grp"), lax.axis_size("shard")
    tok_count, width = tokens.shape
    depth, tile = w_gate.shape[1:]
    chunks, cw = tok_count // CHUNK, width // shards
    half = chunks // 2
    copies = half + 2 + 3 + half + chunks + 1 + 2 + chunks + (shards - 1) * chunks
    lanes = -(-tok_count // 128) * 128
    bf16, f32 = jnp.bfloat16, jnp.float32
    block = (chunks, shards, CHUNK, cw)
    whole = pl.BlockSpec(memory_space=pltpu.VMEM)
    away = pl.BlockSpec(memory_space=pltpu.HBM)
    total_rows = groups * tok_count
    mixed = pl.pallas_call(
        functools.partial(dense_kernel, groups, shards),
        out_shape=jax.ShapeDtypeStruct((chunks, CHUNK, cw), bf16),
        in_specs=[away, whole, whole, away, away, away],
        out_specs=whole,
        scratch_shapes=[
            pltpu.VMEM((4, chunks, CHUNK, width), bf16),
            pltpu.VMEM((4, -(-groups // 8) * 8, lanes), f32),
            pltpu.VMEM((depth, tile), bf16),
            pltpu.VMEM((depth, tile), bf16),
            pltpu.VMEM((tile, width), bf16),
            pltpu.VMEM(block, f32),
            pltpu.VMEM(block, f32),
            pltpu.VMEM((2,) + block, bf16),
            pltpu.VMEM((2,) + block, bf16),
            pltpu.VMEM(block, bf16),
            pltpu.VMEM(block, bf16),
            pltpu.VMEM(block, bf16),
            pltpu.VMEM((shards - 1, chunks, CHUNK, cw), bf16),
            pltpu.SemaphoreType.DMA((5,)),
            pltpu.SemaphoreType.DMA((copies,)),
            pltpu.SemaphoreType.DMA((copies,)),
        ],
        compiler_params=pltpu.CompilerParams(
            collective_id=0, has_side_effects=True, vmem_limit_bytes=60 * 1024 * 1024
        ),
        cost_estimate=pl.CostEstimate(
            flops=6 * total_rows * depth * tile, bytes_accessed=6 * depth * tile, transcendentals=total_rows * tile
        ),
    )(tokens.reshape(chunks, CHUNK, width), routes.T, probs.T, w_gate, w_up, w_down)
    return mixed.reshape(tok_count, cw)


def is_dense(mesh, tokens, routes):
    groups, shards, sides = mesh.shape["grp"], mesh.shape["shard"], mesh.shape["side"]
    tok_count = tokens.shape[0] // (groups * sides)
    per_group = shards // TPE
    capacity = 2 * tok_count * routes.shape[1] // (groups * per_group)
    return groups == 4 and per_group == 1 and capacity >= tok_count and tok_count % (2 * CHUNK) == 0


def solution(mesh):
    def call(tokens, routes, probs, w_gate, w_up, w_down):
        body = dense_on_device if is_dense(mesh, tokens, routes) else on_device
        return jax.shard_map(
            body,
            mesh=mesh,
            in_specs=(
                P(("grp", "side"), None),
                P(("grp", "side"), None),
                P(("grp", "side"), None),
                P(("grp", "shard"), None, None),
                P(("grp", "shard"), None, None),
                P(("grp", "shard"), None, None),
            ),
            out_specs=P(("grp", "side"), "shard"),
            check_vma=False,
        )(tokens, routes, probs, w_gate, w_up, w_down)

    return call
```

```python
import functools

import jax
import jax.numpy as jnp
from jax import lax
from jax.experimental import pallas as pl
from jax.experimental.pallas import tpu as pltpu
from jax.sharding import PartitionSpec as P

TPE = 4
CHUNK = 16
PIECES = 2
MESH = pl.DeviceIdType.MESH


def tile_pass(rows, w_gate, w_up, w_down):
    flat = rows.reshape(-1, rows.shape[2])
    gate = jnp.dot(flat, w_gate[0], preferred_element_type=jnp.float32)
    upper = jnp.dot(flat, w_up[0], preferred_element_type=jnp.float32)
    hidden = (jax.nn.silu(gate) * upper).astype(jnp.bfloat16)
    result = jnp.dot(hidden, w_down[0], preferred_element_type=jnp.float32).astype(jnp.bfloat16)
    return result.reshape(rows.shape[0], rows.shape[1], -1)


def on_device(tokens, routes, probs, w_gate, w_up, w_down):
    groups = lax.axis_size("grp")
    shards = lax.axis_size("shard")
    per_group = shards // TPE
    experts_all = groups * per_group
    tok_count = tokens.shape[0]
    top_count = routes.shape[1]
    capacity = 2 * tok_count * top_count // experts_all
    local = lax.axis_index("shard") // TPE
    targets = jnp.arange(groups, dtype=jnp.int32) * per_group + local
    gates = probs / jnp.sum(probs, axis=-1, keepdims=True)
    match = routes[:, :, None] == targets[None, None, :]
    hits = jnp.sum(match.astype(jnp.int32), axis=1)
    gate_hits = jnp.sum(jnp.where(match, gates[:, :, None], jnp.float32(0.0)), axis=1)
    ranks = jnp.cumsum(hits, axis=0) - 1
    slots = jnp.arange(capacity, dtype=jnp.int32)
    select = ((hits.T[:, None, :] > 0) & (ranks.T[:, None, :] == slots[None, :, None])).astype(
        jnp.bfloat16
    )
    outgoing = jnp.einsum("gct,td->gcd", select, tokens, preferred_element_type=jnp.float32).astype(
        jnp.bfloat16
    )
    arrived = lax.all_to_all(outgoing, "grp", split_axis=0, concat_axis=0, tiled=True)
    results = tile_pass(arrived, w_gate, w_up, w_down)
    returned = lax.all_to_all(results, "grp", split_axis=0, concat_axis=0, tiled=True)

    def add_group(total, items):
        picks, rows_back, weight = items
        picked = jnp.einsum("ct,cd->td", picks, rows_back, preferred_element_type=jnp.float32)
        return (total + weight[:, None] * picked, None)

    start = jnp.zeros((tok_count, tokens.shape[1]), jnp.float32)
    combined, unused = lax.scan(add_group, start, (select, returned, gate_hits.T))
    return lax.psum_scatter(combined, "shard", scatter_dimension=1, tiled=True).astype(jnp.bfloat16)


def dense_kernel(
    groups, shards, tokens, routes, probs, wg_hbm, wu_hbm, wd_hbm, out,
    x, gt, wg, wu, wd, own, cross, lend, borrowed, y_out, y_in, z_out, z_in, local_sem, send_sem, recv_sem,
):
    chunks, rows_per, width = tokens.shape
    half = chunks // 2
    rows = chunks * rows_per
    depth = wg.shape[0]
    grp, z = lax.axis_index("grp"), lax.axis_index("shard")
    odd = lax.rem(z, 2)
    sibling = {"grp": grp + 1 - 2 * lax.rem(grp, 2)}
    over = lax.rem(grp + 2, groups)
    across = {"grp": over}
    diagonal = {"grp": over + 1 - 2 * lax.rem(over, 2)}
    pair = {"shard": z + 1 - 2 * odd}
    rest = [{"shard": lax.rem(z + d, shards)} for d in range(1, shards)]

    loads = [
        pltpu.make_async_copy(wg_hbm.at[0], wg, local_sem.at[0]),
        pltpu.make_async_copy(wu_hbm.at[0], wu, local_sem.at[1]),
        pltpu.make_async_copy(wd_hbm.at[0], wd, local_sem.at[2]),
    ]
    starts = [half * odd, half * (1 - odd)]
    loads += [
        pltpu.make_async_copy(tokens.at[pl.ds(starts[i], half)], x.at[0, pl.ds(i * half, half)], local_sem.at[3 + i])
        for i in range(2)
    ]
    for load in loads:
        load.start()

    barrier = pltpu.get_barrier_semaphore()
    greeted = [sibling, across, diagonal] + rest
    for device in greeted:
        pl.semaphore_signal(barrier, inc=1, device_id=device, device_id_type=MESH)

    share = probs[...] / jnp.sum(probs[...], axis=0, keepdims=True)
    gt[0] = jnp.zeros(gt.shape[1:], jnp.float32)
    for expert in range(groups):
        line = jnp.sum(jnp.where(routes[...] == expert, share, 0.0), axis=0, keepdims=True)
        gt[0, expert : expert + 1, 0:rows] = line

    pl.semaphore_wait(barrier, len(greeted))

    number = [0]

    def remote(from_ref, to_ref, device):
        at = number[0]
        number[0] += 1
        return pltpu.make_async_remote_copy(
            src_ref=from_ref, dst_ref=to_ref, send_sem=send_sem.at[at], recv_sem=recv_sem.at[at],
            device_id=device, device_id_type=MESH,
        )

    sent = []

    def begin(copy):
        copy.start()
        sent.append(copy)
        return copy

    wide = width // PIECES
    spots = [(k, s) for k in range(half) for s in range(PIECES)]

    def spot(ref, lead, k, s):
        return ref.at[lead + (k, slice(None), pl.ds(s * wide, wide))]

    direct = {
        (k, s): begin(remote(spot(tokens, (), half * odd + k, s), spot(x, (2,), k, s), across)) for k, s in spots
    }
    beside = [
        begin(remote(tokens.at[pl.ds(starts[i], half)], x.at[1, pl.ds(i * half, half)], sibling)) for i in range(2)
    ]
    gate_copies = [
        begin(remote(gt.at[0], gt.at[slot], device))
        for slot, device in ((1, sibling), (2, across), (3, diagonal))
    ]
    paired = {(k, s): remote(spot(x, (2,), k, s), spot(x, (2,), half + k, s), pair) for k, s in spots}
    every = [(r, s) for r in range(chunks) for s in range(PIECES)]
    passed = {(r, s): remote(spot(x, (2,), r, s), spot(x, (3,), r, s), sibling) for r, s in every}
    lent_home = remote(lend.at[0], borrowed.at[0], sibling)
    lent_away = {(r, s): remote(lend.at[1, r, s], borrowed.at[1, r, s], sibling) for r, s in every}
    y_copies = {(r, s): remote(y_out.at[r, s], y_in.at[r, s], across) for r, s in every}
    z_base = number[0]

    def z_copy(step, r, s, to_index):
        row = z_base + ((step - 1) * PIECES + s) * chunks
        return pltpu.make_async_remote_copy(
            src_ref=z_out.at[r, s, lax.rem(z + step, shards)],
            dst_ref=z_in.at[step - 1, to_index, s],
            send_sem=send_sem.at[row + r],
            recv_sem=recv_sem.at[row + to_index],
            device_id=rest[step - 1],
            device_id_type=MESH,
        )

    def gate_column(slot, first, count):
        picked = jnp.where(lax.broadcasted_iota(jnp.int32, gt.shape[1:], 0) == grp, gt[slot], 0.0)
        line = jnp.sum(picked, axis=0, keepdims=True)
        at = lax.broadcasted_iota(jnp.int32, (count, gt.shape[2]), 0) + (first + half * rows_per * odd)
        at = lax.rem(at, rows)
        return jnp.sum(
            jnp.where(at == lax.broadcasted_iota(jnp.int32, (count, gt.shape[2]), 1), line, 0.0), axis=1, keepdims=True
        )

    def enter(slot, first, count):
        each = count * rows_per
        steps = 4
        span = depth // steps
        gate = jnp.zeros((2 * each, wg.shape[1]), jnp.float32)
        upper = jnp.zeros((2 * each, wg.shape[1]), jnp.float32)
        for step in range(steps):
            piece = x[slot : slot + 2, first : first + count, :, step * span : (step + 1) * span]
            piece = piece.reshape(2 * each, span)
            gate += jnp.dot(piece, wg[step * span : (step + 1) * span, :], preferred_element_type=jnp.float32)
            upper += jnp.dot(piece, wu[step * span : (step + 1) * span, :], preferred_element_type=jnp.float32)
        hidden = (gate / (1.0 + jnp.exp(-gate)) * upper).astype(jnp.bfloat16)
        scale = jnp.concatenate(
            [gate_column(slot, first * rows_per, each), gate_column(slot + 1, first * rows_per, each)], axis=0
        )
        return hidden, scale

    cw = width // shards
    cs = cw // PIECES

    def leave(entered, first, count, s, kept, given):
        hidden, scale = entered
        each = count * rows_per
        for q in range(shards):
            at = q * cw + s * cs
            part = jnp.dot(hidden, wd[:, at : at + cs], preferred_element_type=jnp.float32) * scale
            kept[first : first + count, s, q] = part[:each].reshape(count, rows_per, cs)
            lend[given, first : first + count, s, q] = part[each:].astype(jnp.bfloat16).reshape(count, rows_per, cs)

    def arrive(k, s):
        direct[k, s].wait_recv()
        begin(paired[k, s])
        begin(passed[k, s])

    def arrive_pair(k, s):
        paired[k, s].wait_recv()
        begin(passed[half + k, s])

    def to_across(r, s):
        lent_away[r, s].wait_recv()
        y_out[r, s] = (cross[r, s] + borrowed[1, r, s].astype(jnp.float32)).astype(jnp.bfloat16)
        begin(y_copies[r, s])

    def settle(r, s):
        y_copies[r, s].wait_recv()
        total = own[r, s] + borrowed[0, r, s].astype(jnp.float32) + y_in[r, s].astype(jnp.float32)
        own[r, s] = total
        z_out[r, s] = total.astype(jnp.bfloat16)
        for step in range(1, shards):
            begin(z_copy(step, r, s, lax.rem(r + half * lax.rem(step, 2), chunks)))

    pieces = range(PIECES)
    for i in (3, 4, 0, 1):
        loads[i].wait()
    for copy in beside + gate_copies:
        copy.wait_recv()
    entered = enter(0, 0, chunks)
    for s in pieces:
        arrive(0, s)
    loads[2].wait()
    for s in pieces:
        leave(entered, 0, chunks, s, own, 0)
    begin(lent_home)
    waiting = [(k, s) for k in range(1, half) for s in pieces]
    later = [(k, s) for k in range(half) for s in pieces]
    settled = list(every)
    for r in range(chunks):
        if r < half:
            for k, s in [spot_ for spot_ in waiting if spot_[0] == r]:
                arrive(k, s)
        else:
            for k, s in [spot_ for spot_ in later if spot_[0] == r - half]:
                arrive_pair(k, s)
        for s in pieces:
            passed[r, s].wait_recv()
        entered = enter(2, r, 1)
        if r > 0:
            for s in pieces:
                to_across(r - 1, s)
        for s in pieces:
            leave(entered, r, 1, s, cross, 1)
            begin(lent_away[r, s])
    lent_home.wait_recv()
    first_settled = settled.pop(0)
    settle(*first_settled)
    for s in pieces:
        to_across(chunks - 1, s)
    for r, s in settled:
        settle(r, s)
    for r in range(chunks):
        for s in pieces:
            total = own[r, s, z]
            for step in range(1, shards):
                z_copy(step, r, s, r).wait_recv()
                total = total + z_in[step - 1, r, s].astype(jnp.float32)
            out[lax.rem(r + half * odd, chunks), :, s * cs : (s + 1) * cs] = total.astype(jnp.bfloat16)
    for copy in sent:
        copy.wait_send()


def dense_on_device(tokens, routes, probs, w_gate, w_up, w_down):
    groups, shards = lax.axis_size("grp"), lax.axis_size("shard")
    tok_count, width = tokens.shape
    depth, tile = w_gate.shape[1:]
    chunks, cw = tok_count // CHUNK, width // shards
    half = chunks // 2
    copies = 2 + 3 + 1 + (2 * half + (3 + shards - 1) * chunks) * PIECES
    lanes = -(-tok_count // 128) * 128
    bf16, f32 = jnp.bfloat16, jnp.float32
    block = (chunks, PIECES, shards, CHUNK, cw // PIECES)
    whole = pl.BlockSpec(memory_space=pltpu.VMEM)
    away = pl.BlockSpec(memory_space=pltpu.HBM)
    total_rows = groups * tok_count
    mixed = pl.pallas_call(
        functools.partial(dense_kernel, groups, shards),
        out_shape=jax.ShapeDtypeStruct((chunks, CHUNK, cw), bf16),
        in_specs=[away, whole, whole, away, away, away],
        out_specs=whole,
        scratch_shapes=[
            pltpu.VMEM((4, chunks, CHUNK, width), bf16),
            pltpu.VMEM((4, -(-groups // 8) * 8, lanes), f32),
            pltpu.VMEM((depth, tile), bf16),
            pltpu.VMEM((depth, tile), bf16),
            pltpu.VMEM((tile, width), bf16),
            pltpu.VMEM(block, f32),
            pltpu.VMEM(block, f32),
            pltpu.VMEM((2,) + block, bf16),
            pltpu.VMEM((2,) + block, bf16),
            pltpu.VMEM(block, bf16),
            pltpu.VMEM(block, bf16),
            pltpu.VMEM(block, bf16),
            pltpu.VMEM((shards - 1, chunks, PIECES, CHUNK, cw // PIECES), bf16),
            pltpu.SemaphoreType.DMA((5,)),
            pltpu.SemaphoreType.DMA((copies,)),
            pltpu.SemaphoreType.DMA((copies,)),
        ],
        compiler_params=pltpu.CompilerParams(
            collective_id=0, has_side_effects=True, vmem_limit_bytes=40 * 1024 * 1024
        ),
        cost_estimate=pl.CostEstimate(
            flops=6 * total_rows * depth * tile, bytes_accessed=6 * depth * tile, transcendentals=total_rows * tile
        ),
    )(tokens.reshape(chunks, CHUNK, width), routes.T, probs.T, w_gate, w_up, w_down)
    return mixed.reshape(tok_count, cw)


def is_dense(mesh, tokens, routes):
    groups, shards, sides = mesh.shape["grp"], mesh.shape["shard"], mesh.shape["side"]
    tok_count = tokens.shape[0] // (groups * sides)
    per_group = shards // TPE
    capacity = 2 * tok_count * routes.shape[1] // (groups * per_group)
    return groups == 4 and per_group == 1 and capacity >= tok_count and tok_count % (2 * CHUNK) == 0 and tokens.shape[1] % (shards * PIECES * 128) == 0


def solution(mesh):
    def call(tokens, routes, probs, w_gate, w_up, w_down):
        body = dense_on_device if is_dense(mesh, tokens, routes) else on_device
        return jax.shard_map(
            body,
            mesh=mesh,
            in_specs=(
                P(("grp", "side"), None),
                P(("grp", "side"), None),
                P(("grp", "side"), None),
                P(("grp", "shard"), None, None),
                P(("grp", "shard"), None, None),
                P(("grp", "shard"), None, None),
            ),
            out_specs=P(("grp", "side"), "shard"),
            check_vma=False,
        )(tokens, routes, probs, w_gate, w_up, w_down)

    return call
```

```python
import functools

import jax
import jax.numpy as jnp
from jax import lax
from jax.experimental import pallas as pl
from jax.experimental.pallas import tpu as pltpu
from jax.sharding import PartitionSpec as P

TPE = 4
CHUNK = 16
PIECES = 2
MESH = pl.DeviceIdType.MESH


def tile_pass(rows, w_gate, w_up, w_down):
    flat = rows.reshape(-1, rows.shape[2])
    gate = jnp.dot(flat, w_gate[0], preferred_element_type=jnp.float32)
    upper = jnp.dot(flat, w_up[0], preferred_element_type=jnp.float32)
    hidden = (jax.nn.silu(gate) * upper).astype(jnp.bfloat16)
    result = jnp.dot(hidden, w_down[0], preferred_element_type=jnp.float32).astype(jnp.bfloat16)
    return result.reshape(rows.shape[0], rows.shape[1], -1)


def on_device(tokens, routes, probs, w_gate, w_up, w_down):
    groups = lax.axis_size("grp")
    shards = lax.axis_size("shard")
    per_group = shards // TPE
    experts_all = groups * per_group
    tok_count = tokens.shape[0]
    top_count = routes.shape[1]
    capacity = 2 * tok_count * top_count // experts_all
    local = lax.axis_index("shard") // TPE
    targets = jnp.arange(groups, dtype=jnp.int32) * per_group + local
    gates = probs / jnp.sum(probs, axis=-1, keepdims=True)
    match = routes[:, :, None] == targets[None, None, :]
    hits = jnp.sum(match.astype(jnp.int32), axis=1)
    gate_hits = jnp.sum(jnp.where(match, gates[:, :, None], jnp.float32(0.0)), axis=1)
    ranks = jnp.cumsum(hits, axis=0) - 1
    slots = jnp.arange(capacity, dtype=jnp.int32)
    select = ((hits.T[:, None, :] > 0) & (ranks.T[:, None, :] == slots[None, :, None])).astype(
        jnp.bfloat16
    )
    outgoing = jnp.einsum("gct,td->gcd", select, tokens, preferred_element_type=jnp.float32).astype(
        jnp.bfloat16
    )
    arrived = lax.all_to_all(outgoing, "grp", split_axis=0, concat_axis=0, tiled=True)
    results = tile_pass(arrived, w_gate, w_up, w_down)
    returned = lax.all_to_all(results, "grp", split_axis=0, concat_axis=0, tiled=True)

    def add_group(total, items):
        picks, rows_back, weight = items
        picked = jnp.einsum("ct,cd->td", picks, rows_back, preferred_element_type=jnp.float32)
        return (total + weight[:, None] * picked, None)

    start = jnp.zeros((tok_count, tokens.shape[1]), jnp.float32)
    combined, unused = lax.scan(add_group, start, (select, returned, gate_hits.T))
    return lax.psum_scatter(combined, "shard", scatter_dimension=1, tiled=True).astype(jnp.bfloat16)


def dense_kernel(
    groups, shards, tokens, routes, probs, wg_hbm, wu_hbm, wd_hbm, out,
    x, gt, wg, wu, wd, own, cross, lend, borrowed, y_out, y_in, z_out, z_in, local_sem, send_sem, recv_sem,
):
    chunks, rows_per, width = tokens.shape
    half = chunks // 2
    rows = chunks * rows_per
    depth = wg.shape[0]
    grp, z = lax.axis_index("grp"), lax.axis_index("shard")
    odd = lax.rem(z, 2)
    sibling = {"grp": grp + 1 - 2 * lax.rem(grp, 2)}
    over = lax.rem(grp + 2, groups)
    across = {"grp": over}
    diagonal = {"grp": over + 1 - 2 * lax.rem(over, 2)}
    pair = {"shard": z + 1 - 2 * odd}
    rest = [{"shard": lax.rem(z + d, shards)} for d in range(1, shards)]

    loads = [
        pltpu.make_async_copy(wg_hbm.at[0], wg, local_sem.at[0]),
        pltpu.make_async_copy(wu_hbm.at[0], wu, local_sem.at[1]),
        pltpu.make_async_copy(wd_hbm.at[0], wd, local_sem.at[2]),
    ]
    starts = [half * odd, half * (1 - odd)]
    loads += [
        pltpu.make_async_copy(tokens.at[pl.ds(starts[i], half)], x.at[0, pl.ds(i * half, half)], local_sem.at[3 + i])
        for i in range(2)
    ]
    for load in loads:
        load.start()

    barrier = pltpu.get_barrier_semaphore()
    greeted = [sibling, across, diagonal] + rest
    for device in greeted:
        pl.semaphore_signal(barrier, inc=1, device_id=device, device_id_type=MESH)

    share = probs[...] / jnp.sum(probs[...], axis=0, keepdims=True)
    gt[0] = jnp.zeros(gt.shape[1:], jnp.float32)
    for expert in range(groups):
        line = jnp.sum(jnp.where(routes[...] == expert, share, 0.0), axis=0, keepdims=True)
        gt[0, expert : expert + 1, 0:rows] = line

    pl.semaphore_wait(barrier, len(greeted))

    number = [0]

    def remote(from_ref, to_ref, device):
        at = number[0]
        number[0] += 1
        return pltpu.make_async_remote_copy(
            src_ref=from_ref, dst_ref=to_ref, send_sem=send_sem.at[at], recv_sem=recv_sem.at[at],
            device_id=device, device_id_type=MESH,
        )

    sent = []

    def begin(copy):
        copy.start()
        sent.append(copy)
        return copy

    wide = width // PIECES
    spots = [(k, s) for k in range(half) for s in range(PIECES)]

    def spot(ref, lead, k, s):
        return ref.at[lead + (k, slice(None), pl.ds(s * wide, wide))]

    direct = {
        (k, s): begin(remote(spot(tokens, (), half * odd + k, s), spot(x, (2,), k, s), across)) for k, s in spots
    }
    beside = [
        begin(remote(tokens.at[pl.ds(starts[i], half)], x.at[1, pl.ds(i * half, half)], sibling)) for i in range(2)
    ]
    gate_copies = [
        begin(remote(gt.at[0], gt.at[slot], device))
        for slot, device in ((1, sibling), (2, across), (3, diagonal))
    ]
    paired = {(k, s): remote(spot(x, (2,), k, s), spot(x, (2,), half + k, s), pair) for k, s in spots}
    every = [(r, s) for r in range(chunks) for s in range(PIECES)]
    passed = {(r, s): remote(spot(x, (2,), r, s), spot(x, (3,), r, s), sibling) for r, s in every}
    lent_home = remote(lend.at[0], borrowed.at[0], sibling)
    passes = [(0, 1), (1, chunks - 2), (chunks - 1, 1)]
    lent_away = [
        remote(lend.at[1, pl.ds(first, count)], borrowed.at[1, pl.ds(first, count)], sibling)
        for first, count in passes
    ]
    units = [(r, 0, PIECES) for r in range(chunks - 1)] + [(chunks - 1, s, 1) for s in range(PIECES)]
    y_copies = {(r, s): remote(y_out.at[r, pl.ds(s, n)], y_in.at[r, pl.ds(s, n)], across) for r, s, n in units}
    z_base = number[0]

    def z_copy(step, r, s, n, to_index):
        row = z_base + ((step - 1) * PIECES + s) * chunks
        return pltpu.make_async_remote_copy(
            src_ref=z_out.at[r, lax.rem(z + step, shards), pl.ds(s, n)],
            dst_ref=z_in.at[step - 1, to_index, pl.ds(s, n)],
            send_sem=send_sem.at[row + r],
            recv_sem=recv_sem.at[row + to_index],
            device_id=rest[step - 1],
            device_id_type=MESH,
        )

    def gate_column(slot, first, count):
        picked = jnp.where(lax.broadcasted_iota(jnp.int32, gt.shape[1:], 0) == grp, gt[slot], 0.0)
        line = jnp.sum(picked, axis=0, keepdims=True)
        at = lax.broadcasted_iota(jnp.int32, (count, gt.shape[2]), 0) + (first + half * rows_per * odd)
        at = lax.rem(at, rows)
        return jnp.sum(
            jnp.where(at == lax.broadcasted_iota(jnp.int32, (count, gt.shape[2]), 1), line, 0.0), axis=1, keepdims=True
        )

    def enter(parts):
        steps = 4
        span = depth // steps
        gate = upper = 0.0
        for step in range(steps):
            at = slice(step * span, (step + 1) * span)
            piece = jnp.concatenate(
                [x[slot : slot + 2, a : a + n, :, at].reshape(2 * n * rows_per, span) for slot, a, n in parts], axis=0
            )
            gate += jnp.dot(piece, wg[at, :], preferred_element_type=jnp.float32)
            upper += jnp.dot(piece, wu[at, :], preferred_element_type=jnp.float32)
        hidden = (gate / (1.0 + jnp.exp(-gate)) * upper).astype(jnp.bfloat16)
        scale = jnp.concatenate(
            [gate_column(slot + i, a * rows_per, n * rows_per) for slot, a, n in parts for i in range(2)], axis=0
        )
        return hidden, scale

    cw = width // shards
    cs = cw // PIECES

    def leave(entered, parts):
        hidden, scale = entered
        for s in range(PIECES):
            for q in range(shards):
                at = q * cw + s * cs
                part = jnp.dot(hidden, wd[:, at : at + cs], preferred_element_type=jnp.float32) * scale
                base = 0
                for slot, a, n in parts:
                    each = n * rows_per
                    mine, other = part[base : base + each], part[base + each : base + 2 * each]
                    base += 2 * each
                    lent = other.astype(jnp.bfloat16).reshape(n, rows_per, cs)
                    kept, given = (own, 0) if slot == 0 else (cross, 1)
                    kept[a : a + n, s, q] = mine.reshape(n, rows_per, cs)
                    lend[given, a : a + n, s, q] = lent

    def arrive(k, s):
        direct[k, s].wait_recv()
        begin(paired[k, s])
        begin(passed[k, s])

    def arrive_pair(k, s):
        paired[k, s].wait_recv()
        begin(passed[half + k, s])

    def to_across(r):
        y_out[r] = (cross[r] + borrowed[1, r].astype(jnp.float32)).astype(jnp.bfloat16)
        for s in sorted(s for chunk, s in y_copies if chunk == r):
            begin(y_copies[r, s])

    def settle(r, s, n):
        y_copies[r, s].wait_recv()
        for i in range(s, s + n):
            total = own[r, i] + borrowed[0, r, i].astype(jnp.float32) + y_in[r, i].astype(jnp.float32)
            own[r, i] = total
            for q in range(shards):
                z_out[r, q, i] = total[q].astype(jnp.bfloat16)
        for step in range(1, shards):
            begin(z_copy(step, r, s, n, (r + half * (step % 2)) % chunks))

    pieces = range(PIECES)
    for i in (3, 4, 0, 1):
        loads[i].wait()
    for copy in beside + gate_copies:
        copy.wait_recv()
    for s in pieces:
        arrive(0, s)
    for s in pieces:
        passed[0, s].wait_recv()
    parts = [(0, 0, chunks), (2, 0, 1)]
    entered = enter(parts)
    for k in range(1, half):
        for s in pieces:
            arrive(k, s)
    loads[2].wait()
    leave(entered, parts)
    begin(lent_away[0])
    begin(lent_home)
    for k in range(half - 1):
        for s in pieces:
            arrive_pair(k, s)
    lent_away[0].wait_recv()
    to_across(0)
    for r in range(1, chunks - 1):
        for s in pieces:
            passed[r, s].wait_recv()
    parts = [(2, 1, chunks - 2)]
    entered = enter(parts)
    for s in pieces:
        arrive_pair(half - 1, s)
    leave(entered, parts)
    begin(lent_away[1])
    for s in pieces:
        passed[chunks - 1, s].wait_recv()
    parts = [(2, chunks - 1, 1)]
    lent_away[1].wait_recv()
    for r in range(1, chunks - 1):
        to_across(r)
    entered = enter(parts)
    lent_home.wait_recv()
    settle(*units[0])
    leave(entered, parts)
    begin(lent_away[2])
    lent_away[2].wait_recv()
    to_across(chunks - 1)
    for unit in units[1:]:
        settle(*unit)
    for r, s, n in units:
        for step in range(1, shards):
            z_copy(step, r, s, n, (r + half * (step % 2)) % chunks).wait_recv()
    for r in range(chunks):
        for i in pieces:
            total = own[r, i, z]
            for step in range(1, shards):
                total = total + z_in[step - 1, r, i].astype(jnp.float32)
            out[lax.rem(r + half * odd, chunks), :, i * cs : (i + 1) * cs] = total.astype(jnp.bfloat16)
    for copy in sent:
        copy.wait_send()


def dense_on_device(tokens, routes, probs, w_gate, w_up, w_down):
    groups, shards = lax.axis_size("grp"), lax.axis_size("shard")
    tok_count, width = tokens.shape
    depth, tile = w_gate.shape[1:]
    chunks, cw = tok_count // CHUNK, width // shards
    half = chunks // 2
    copies = 2 + 3 + 1 + (2 * half + (3 + shards - 1) * chunks) * PIECES
    lanes = -(-tok_count // 128) * 128
    bf16, f32 = jnp.bfloat16, jnp.float32
    block = (chunks, PIECES, shards, CHUNK, cw // PIECES)
    whole = pl.BlockSpec(memory_space=pltpu.VMEM)
    away = pl.BlockSpec(memory_space=pltpu.HBM)
    total_rows = groups * tok_count
    mixed = pl.pallas_call(
        functools.partial(dense_kernel, groups, shards),
        out_shape=jax.ShapeDtypeStruct((chunks, CHUNK, cw), bf16),
        in_specs=[away, whole, whole, away, away, away],
        out_specs=whole,
        scratch_shapes=[
            pltpu.VMEM((4, chunks, CHUNK, width), bf16),
            pltpu.VMEM((4, -(-groups // 8) * 8, lanes), f32),
            pltpu.VMEM((depth, tile), bf16),
            pltpu.VMEM((depth, tile), bf16),
            pltpu.VMEM((tile, width), bf16),
            pltpu.VMEM(block, f32),
            pltpu.VMEM(block, f32),
            pltpu.VMEM((2,) + block, bf16),
            pltpu.VMEM((2,) + block, bf16),
            pltpu.VMEM(block, bf16),
            pltpu.VMEM(block, bf16),
            pltpu.VMEM((chunks, shards, PIECES, CHUNK, cw // PIECES), bf16),
            pltpu.VMEM((shards - 1, chunks, PIECES, CHUNK, cw // PIECES), bf16),
            pltpu.SemaphoreType.DMA((5,)),
            pltpu.SemaphoreType.DMA((copies,)),
            pltpu.SemaphoreType.DMA((copies,)),
        ],
        compiler_params=pltpu.CompilerParams(
            collective_id=0, has_side_effects=True, vmem_limit_bytes=60 * 1024 * 1024
        ),
        cost_estimate=pl.CostEstimate(
            flops=6 * total_rows * depth * tile, bytes_accessed=6 * depth * tile, transcendentals=total_rows * tile
        ),
    )(tokens.reshape(chunks, CHUNK, width), routes.T, probs.T, w_gate, w_up, w_down)
    return mixed.reshape(tok_count, cw)


def is_dense(mesh, tokens, routes):
    groups, shards, sides = mesh.shape["grp"], mesh.shape["shard"], mesh.shape["side"]
    tok_count = tokens.shape[0] // (groups * sides)
    per_group = shards // TPE
    capacity = 2 * tok_count * routes.shape[1] // (groups * per_group)
    return groups == 4 and per_group == 1 and capacity >= tok_count and tok_count % (4 * CHUNK) == 0 and tokens.shape[1] % (shards * PIECES * 128) == 0


def solution(mesh):
    def call(tokens, routes, probs, w_gate, w_up, w_down):
        body = dense_on_device if is_dense(mesh, tokens, routes) else on_device
        return jax.shard_map(
            body,
            mesh=mesh,
            in_specs=(
                P(("grp", "side"), None),
                P(("grp", "side"), None),
                P(("grp", "side"), None),
                P(("grp", "shard"), None, None),
                P(("grp", "shard"), None, None),
                P(("grp", "shard"), None, None),
            ),
            out_specs=P(("grp", "side"), "shard"),
            check_vma=False,
        )(tokens, routes, probs, w_gate, w_up, w_down)

    return call
```
